32 devices in a mesh: band: 8 (over z, x), slab: 4 (over y, core).
Axes of the slice: x: 2, y: 2, z: 4, core: 2. Of those that a mesh axis runs over, the one named last changes fastest.
Arguments:
- orbitals: float32 [32, 128, 128, 128], P('band', 'slab'), may hold values from -6 to 6
- owner_band: int32 [4], replicated, may hold values from 0 to 7
- owner_slot: int32 [4], replicated, may hold values from 0 to 3
- g_mask: int32 [128, 128, 128], P(None, 'slab'), may hold values from 0 to 1, as said below
Outputs:
- exchange_action: float32 [32, 128, 128, 128], P('band', 'slab')
The draws below stay inside these ranges and needn't reach their ends.
Inputs may be any that keep to these rules, and one draw needn't show every extreme that they name: `owner_band`: the band index of the device that holds source orbital j. `owner_slot`: the position of source orbital j among its owner's 4 orbitals. 1 where the kernel is kept and 0 where it is cut; the point of zero wave vector, g_mask[0, 0, 0], is always cut.
All inputs are finite; a program needn't handle non-finite values.
Results may differ from the reference program's by a relative error of at most 0.0003.
Values sent between devices are 32-bit elements; how exact they have to be, the bound alone decides.
A program may use at most 192 MiB of HBM per device.

```python
import math
import jax
import jax.numpy as jnp
from jax import lax

GRID = 128
ORB_DEV = 4
NSRC = 4
NORB = 32
N_BAND = 8


def draw_g_mask(key, part):
    draws = jax.random.randint(key, (GRID, GRID, GRID), 0, 20, dtype=jnp.int32)
    wave_index = jnp.arange(GRID, dtype=jnp.int32)
    folded = jnp.where(wave_index < GRID // 2, wave_index, wave_index - GRID)
    near_axis = jnp.abs(folded) < GRID // 4
    limits = jnp.where(near_axis, 19, 4).astype(jnp.int32)[:, None, None]
    kept = (draws < limits).astype(jnp.int32)
    anchor = (wave_index[:, None, None] == 0) & (wave_index[None, :, None] == 0) & (wave_index[None, None, :] == 0)
    return jnp.where(anchor, 0, kept).astype(jnp.int32)


def place_ends(values, stream_key, least, high):
    dims = values.shape
    place = [jax.random.randint(jax.random.fold_in(stream_key, axis), (), 0, dims[axis]) for axis in range(len(dims))]
    values = values.at[tuple(place)].set(least)
    longest = dims.index(max(dims))
    place[longest] = (place[longest] + 1) % dims[longest]
    return values.at[tuple(place)].set(high)


def block_levels(stream_key, extent, pieces, least, largest):
    factor_of, own = 1.0, jax.random.fold_in(stream_key, 6)
    for axis_at, shards_of in pieces:
        heights = jnp.exp(jax.random.uniform(jax.random.fold_in(own, axis_at), (shards_of,), jnp.float32, least / len(pieces), largest / len(pieces)))
        factor_of = factor_of * jnp.repeat(heights, extent[axis_at] // shards_of).reshape([-1 if axis == axis_at else 1 for axis in range(len(extent))])
    return factor_of


def bell_draw(key, shape, width, limit, pieces=(), kind=jnp.bfloat16):
    entries = width * jax.random.normal(key, shape, jnp.float32)
    if pieces:
        entries = entries * block_levels(key, shape, pieces, -0.22, 0.18)
    return jnp.clip(entries, -limit, limit).astype(kind)


def setup_inputs(seed: int = 0) -> dict:
    splits = jax.random.split(jax.random.key(seed), 5)
    orbitals = bell_draw(splits[0], (NORB, GRID, GRID, GRID), 1.0, 6.0, ((0, 8), (1, 4)), jnp.float32)
    owner_band = place_ends(jax.random.randint(splits[1], (NSRC,), 0, N_BAND), jax.random.fold_in(splits[1], 1), 0, N_BAND - 1).astype(jnp.int32)
    owner_slot = place_ends(jax.random.randint(splits[2], (NSRC,), 0, ORB_DEV), jax.random.fold_in(splits[2], 1), 0, ORB_DEV - 1).astype(jnp.int32)
    g_mask = draw_g_mask(jax.random.fold_in(splits[4], 71), 0)
    return dict(orbitals=orbitals, owner_band=owner_band, owner_slot=owner_slot, g_mask=g_mask)


coulomb_gain = 128.0 * math.pi


def cas_matrix(count):
    wave_index = jnp.arange(count, dtype=jnp.int32)
    products = (wave_index[:, None] * wave_index[None, :]) % count
    angles = (2.0 * math.pi / count) * products.astype(jnp.float32)
    return jnp.cos(angles) + jnp.sin(angles)


def coulomb_field(g_mask):
    wave_index = jnp.arange(GRID, dtype=jnp.int32)
    folded = jnp.where(wave_index < GRID // 2, wave_index, wave_index - GRID).astype(jnp.float32)
    squares = folded[:, None, None] ** 2 + folded[None, :, None] ** 2 + folded[None, None, :] ** 2
    return g_mask.astype(jnp.float32) * coulomb_gain / (squares + 1.0)


def transform_all(field, cas_rows):
    highest = lax.Precision.HIGHEST
    field = jnp.einsum("xyz,kz->xyk", field, cas_rows, precision=highest)
    field = jnp.einsum("xyz,ky->xkz", field, cas_rows, precision=highest)
    return jnp.einsum("xyz,kx->kyz", field, cas_rows, precision=highest)


def reference(orbitals, owner_band, owner_slot, g_mask):
    cas_rows = cas_matrix(GRID)
    coulomb = coulomb_field(g_mask)
    source_ids = (owner_band * ORB_DEV + owner_slot).astype(jnp.int32)
    sources = orbitals[source_ids]
    inverse = 1.0 / (GRID * GRID * GRID)

    def one_target(target):
        def per_source(accumulated, source_field):
            density = target * source_field
            spectrum = transform_all(density, cas_rows)
            potential = transform_all(spectrum * coulomb, cas_rows) * inverse
            return accumulated - potential * source_field, None

        start = jnp.zeros(target.shape, jnp.float32)
        accumulated, _ = lax.scan(per_source, start, sources)
        return accumulated

    return lax.map(one_target, orbitals)
```

```python
import functools
import math

import jax
import jax.numpy as jnp
from jax import lax
from jax.experimental import pallas as pl
from jax.experimental.pallas import tpu as pltpu
from jax.sharding import PartitionSpec as P

GRID = 128


coulomb_gain = 128.0 * math.pi


def broadcast(value, axis, source):
    kept = jnp.where(lax.axis_index(axis) == source, value, 0).astype(value.dtype)
    return lax.psum(kept, axis)


def cas_matrix(count):
    wave_index = jnp.arange(count, dtype=jnp.int32)
    products = wave_index[:, None] * wave_index[None, :] % count
    angles = 2.0 * math.pi / count * products.astype(jnp.float32)
    return jnp.cos(angles) + jnp.sin(angles)


def fold_index(wave_index):
    return jnp.where(wave_index < GRID // 2, wave_index, wave_index - GRID).astype(jnp.float32)


def transform_planes(field, cas_rows):
    highest = lax.Precision.HIGHEST
    field = jnp.einsum("oxyz,kz->oxyk", field, cas_rows, precision=highest)
    return jnp.einsum("oxyz,ky->oxkz", field, cas_rows, precision=highest)


def transform_first(field, cas_rows):
    return jnp.einsum("oxyz,kx->okyz", field, cas_rows, precision=lax.Precision.HIGHEST)


def fetch_source(orbitals, owner_band, owner_slot, which):
    local_copy = lax.dynamic_index_in_dim(orbitals, owner_slot[which], 0, keepdims=False)
    return broadcast(local_copy, "band", owner_band[which])


def per_device(orbitals, owner_band, owner_slot, g_mask):
    cas_rows = cas_matrix(GRID)
    columns_dev = g_mask.shape[1]
    full_index = jnp.arange(GRID, dtype=jnp.int32)
    column_index = lax.axis_index("slab") * columns_dev + jnp.arange(columns_dev, dtype=jnp.int32)
    first_sq = fold_index(full_index) ** 2
    second_sq = fold_index(column_index) ** 2
    squares = first_sq[:, None, None] + second_sq[None, :, None] + first_sq[None, None, :]
    coulomb = g_mask.astype(jnp.float32) * coulomb_gain / (squares + 1.0)
    inverse = 1.0 / (GRID * GRID * GRID)
    source_count = owner_band.shape[0]
    sources = jnp.stack(
        [fetch_source(orbitals, owner_band, owner_slot, which) for which in range(source_count)]
    )
    accumulated = jnp.zeros(orbitals.shape, jnp.float32)
    for which in range(source_count):
        source_field = sources[which]
        density = orbitals * source_field[None]
        spectrum = transform_planes(density, cas_rows)
        items = lax.all_to_all(spectrum, "slab", split_axis=2, concat_axis=1, tiled=True)
        weigh_spectrum = transform_first(items, cas_rows) * coulomb[None]
        potential = transform_first(weigh_spectrum, cas_rows)
        potential = lax.all_to_all(potential, "slab", split_axis=1, concat_axis=2, tiled=True)
        potential = transform_planes(potential, cas_rows) * inverse
        accumulated = accumulated - potential * source_field[None]
    return accumulated


def split_halves(value):
    high = value.astype(jnp.bfloat16)
    low = (value - high.astype(jnp.float32)).astype(jnp.bfloat16)
    return high, low


def split_table(cas):
    high = lax.reduce_precision(cas, 8, 7)
    return high.astype(jnp.bfloat16), (cas - high).astype(jnp.bfloat16)


def right_table(cas):
    high, low = split_table(cas)
    upper = jnp.concatenate([high, low], axis=1)
    lower = jnp.concatenate([high, jnp.zeros_like(low)], axis=1)
    return jnp.concatenate([upper, lower], axis=0)


def left_table(cas):
    high, low = split_table(cas)
    upper = jnp.concatenate([high, high], axis=1)
    lower = jnp.concatenate([low, jnp.zeros_like(low)], axis=1)
    return jnp.concatenate([upper, lower], axis=0)


def apply_right(rows, table):
    high, low = split_halves(rows)
    out = jnp.dot(jnp.concatenate([high, low], axis=1), table, preferred_element_type=jnp.float32)
    return out[:, :GRID] + out[:, GRID:]


def apply_left(table, pair):
    high, low = split_halves(pair)
    out = jnp.dot(table, jnp.concatenate([high, low], axis=0), preferred_element_type=jnp.float32)
    return out[:GRID] + out[GRID:]


STEPS = 8
PLANES = GRID // STEPS


def source_kernel(first, *refs):
    if first:
        target, source, coulomb, zt, yt, xt, yi, xi, out, field = refs
        prior = None
    else:
        target, source, coulomb, zt, yt, xt, yi, xi, prior, out, field = refs
    step = pl.program_id(0)

    @pl.when(step < STEPS)
    def _():
        def pair(p, carry):
            base = pl.multiple_of(p * 2 * GRID, 2 * GRID)
            rows = target[pl.ds(base, 2 * GRID), :] * source[pl.ds(base, 2 * GRID), :]
            rows = apply_right(rows, zt[...])
            both = jnp.concatenate([rows[:GRID], rows[GRID:]], axis=1)
            both = apply_left(yt[...], both)
            plane = step * PLANES + p * 2
            field[pl.ds(plane, GRID, stride=GRID), :] = both[:, :GRID]
            field[pl.ds(plane + 1, GRID, stride=GRID), :] = both[:, GRID:]
            return carry

        lax.fori_loop(0, PLANES // 2, pair, 0, unroll=True)

    @pl.when((step >= STEPS) & (step < 2 * STEPS))
    def _():
        def pair(p, carry):
            base = pl.multiple_of(((step - STEPS) * PLANES + p * 2) * GRID, 2 * GRID)
            local = pl.multiple_of(p * 2 * GRID, 2 * GRID)
            both = jnp.concatenate([field[pl.ds(base, GRID), :], field[pl.ds(base + GRID, GRID), :]], axis=1)
            weight = jnp.concatenate([coulomb[pl.ds(local, GRID), :], coulomb[pl.ds(local + GRID, GRID), :]], axis=1)
            both = apply_left(xt[...], both) * weight
            both = apply_left(xi[...], both)
            field[pl.ds(base, GRID), :] = both[:, :GRID]
            field[pl.ds(base + GRID, GRID), :] = both[:, GRID:]
            return carry

        lax.fori_loop(0, PLANES // 2, pair, 0, unroll=True)

    @pl.when(step >= 2 * STEPS)
    def _():
        def pair(p, carry):
            plane = (step - 2 * STEPS) * PLANES + p * 2
            base = pl.multiple_of(p * 2 * GRID, 2 * GRID)
            both = jnp.concatenate(
                [field[pl.ds(plane, GRID, stride=GRID), :], field[pl.ds(plane + 1, GRID, stride=GRID), :]], axis=1
            )
            both = apply_left(yi[...], both)
            rows = jnp.concatenate([both[:, :GRID], both[:, GRID:]], axis=0)
            rows = apply_right(rows, zt[...]) * source[pl.ds(base, 2 * GRID), :]
            if not first:
                rows = rows + prior[pl.ds(base, 2 * GRID), :]
            out[pl.ds(base, 2 * GRID), :] = rows
            return carry

        lax.fori_loop(0, PLANES // 2, pair, 0, unroll=True)


def add_source(target, source, coulomb, tables, prior):
    rows = PLANES * GRID
    block = lambda index: pl.BlockSpec((rows, GRID), index)
    whole = pl.BlockSpec((2 * GRID, 2 * GRID), lambda i: (0, 0))
    last = STEPS - 1
    begin = lambda i: (jnp.minimum(i, last), 0)
    middle = lambda i: (jnp.clip(i - STEPS, 0, last), 0)
    end = lambda i: (jnp.maximum(i - 2 * STEPS, 0), 0)
    ends = lambda i: (jnp.where(i < 2 * STEPS, jnp.minimum(i, last), i - 2 * STEPS), 0)
    first = prior is None
    specs = [block(begin), block(ends), block(middle)] + [whole] * 5
    operands = [target, source, coulomb] + list(tables)
    if not first:
        specs.append(block(end))
        operands.append(prior)
    cells = GRID * GRID
    return pl.pallas_call(
        functools.partial(source_kernel, first),
        grid=(3 * STEPS,),
        in_specs=specs,
        out_specs=block(end),
        out_shape=jax.ShapeDtypeStruct((cells, GRID), jnp.float32),
        scratch_shapes=[pltpu.VMEM((cells, GRID), jnp.float32)],
        compiler_params=pltpu.CompilerParams(vmem_limit_bytes=48 * 1024 * 1024),
        cost_estimate=pl.CostEstimate(
            flops=6 * 2 * 4 * cells * GRID * GRID, bytes_accessed=5 * 4 * cells * GRID, transcendentals=0
        ),
    )(*operands)


def swap_slab(value, bits):
    return lax.ppermute(value, "slab", [(s, s ^ bits) for s in range(4)])


GROUP = 2


def per_device_whole(orbitals, owner_band, owner_slot, g_mask):
    band, slab = lax.axis_index("band"), lax.axis_index("slab")
    depth = orbitals.shape[1]
    cas = cas_matrix(GRID)
    order = jnp.arange(GRID, dtype=jnp.int32)
    order = ((order // depth) ^ slab) * depth + order % depth
    cas_order = cas[order]
    yt, yi = left_table(cas_order), left_table(cas_order.T)
    tables = (right_table(cas), yt, yi, yi, yt)

    targets = [lax.dynamic_index_in_dim(orbitals, slab ^ r, 0, keepdims=False) for r in range(4)]
    targets = [targets[0]] + [swap_slab(targets[r], r) for r in (1, 2, 3)]
    target = jnp.concatenate(targets, axis=0).reshape(GRID * GRID, GRID)

    full_index = jnp.arange(GRID, dtype=jnp.int32)
    column_index = slab * depth + jnp.arange(depth, dtype=jnp.int32)
    first_sq = fold_index(full_index) ** 2
    second_sq = fold_index(column_index) ** 2
    squares = first_sq[:, None, None] + second_sq[None, :, None] + first_sq[None, None, :]
    gain = -coulomb_gain / (GRID * GRID * GRID)
    weight = (g_mask.astype(jnp.float32) * gain / (squares + 1.0)).transpose(1, 0, 2)
    over = swap_slab(weight, 2)
    near = jnp.concatenate([weight, swap_slab(weight, 1), over, swap_slab(over, 1)], axis=0)
    coulomb = near.reshape(GRID * GRID, GRID)

    result = None
    count = owner_band.shape[0]
    for start in range(0, count, GROUP):
        mine = jnp.stack(
            [
                jnp.where(
                    owner_band[which] == band,
                    lax.dynamic_index_in_dim(orbitals, owner_slot[which], 0, keepdims=False),
                    0.0,
                )
                for which in range(start, start + GROUP)
            ]
        )
        spread = lax.psum(mine, "band")
        for at in range(GROUP):
            own = spread[at]
            far = swap_slab(own, 2)
            pieces = [own, swap_slab(own, 1), far, swap_slab(far, 1)]
            source = jnp.concatenate(pieces, axis=0).reshape(GRID * GRID, GRID)
            result = add_source(target, source, coulomb, tables, result)
    result = result.reshape(4, depth, GRID, GRID)
    parts = [result[0]] + [swap_slab(result[r], r) for r in (1, 2, 3)]
    stacked = jnp.stack(parts, axis=0)
    pairs = stacked.reshape(2, 2, depth, GRID, GRID)
    pairs = jnp.where(slab % 2 == 1, pairs[:, ::-1], pairs)
    pairs = jnp.where(slab // 2 == 1, pairs[::-1], pairs)
    return pairs.reshape(orbitals.shape)


def solution(mesh):
    fits = mesh.shape["band"] == 8 and mesh.shape["slab"] == 4
    return jax.shard_map(
        per_device_whole if fits else per_device,
        mesh=mesh,
        in_specs=(P("band", "slab", None, None), P(), P(), P(None, "slab", None)),
        out_specs=P("band", "slab", None, None),
        check_vma=False,
    )
```
